32 devices in a mesh: groups: 2 (over x), row: 4 (over y, core), col: 4 (over z).
Axes of the slice: x: 2, y: 2, z: 4, core: 2. Of those that a mesh axis runs over, the one named last changes fastest.
Arguments:
- positions: float32 [3, 32768], P(None, ('groups', 'row', 'col')), parts along dimension 1, may hold values from -6 to 6
- strengths: float32 [3, 32768], P(None, ('groups', 'row', 'col')), parts along dimension 1, may hold values from -6 to 6
- cores: float32 [32768], P(('groups', 'row', 'col')), parts along dimension 0, may hold values from 0.3 to 1
- order: int32 [32768], P(('groups', 'row', 'col')), parts along dimension 0, may hold values from 0 to 1023, as said below
- tile_counts: int32 [256], P(('groups', 'row', 'col')), parts along dimension 0, may hold values from 32 to 128
- pair_slots: int32 [2, 2048], P(None, ('groups', 'row', 'col')), parts along dimension 1, may hold values from 0 to 31, as said below
- pair_count: int32 [32], P(('groups', 'row', 'col')), parts along dimension 0, may hold values from 16 to 64, as said below
Outputs:
- velocity: float32 [3, 32768], P(None, ('groups', 'row', 'col')), parts along dimension 1
- stretching: float32 [3, 32768], P(None, ('groups', 'row', 'col')), parts along dimension 1
The draws below stay inside these ranges and needn't reach their ends.
There are 2 independent parts, one for each index of `groups`. The reference program is written for one: setup_inputs(seed, part) draws one part's arguments, and reference() takes and returns one part's arrays. A program takes and returns all parts, laid end to end along the dimension named above; each array names one. Nothing has to cross between parts.
Inputs may be any that keep to these rules, and one draw needn't show every extreme that they name: `order`: each device's block of 1024 entries is a permutation of 0 to 1023. `pair_slots`: row 0 is below 32, row 1 below 32; the first 8 slots of every device pair each of its own tiles with itself. `pair_count`: some device has all its slots live.
All inputs are finite; a program needn't handle non-finite values.
Results may differ from the reference program's by a relative error of at most 0.0001.
Values sent between devices are 32-bit elements; how exact they have to be, the bound alone decides.
A program may use at most 64 MiB of HBM per device.

```python
import math
import jax
import jax.numpy as jnp
from jax import lax

TILE = 128
TILES_DEV = 8
PAIRS_DEV = 64
PAIR_BLOCK = 8
GRID = 16
TILES = 128
NPART = 16384
ROW_TILES = 32
COL_TILES = 32
SLOTS = 1024
N_COL = 4


def draw_order(key, part):
    per_dev = TILES_DEV * TILE
    count = NPART // per_dev
    keys = jax.random.split(jax.random.fold_in(key, 11), count)
    perms = jax.vmap(lambda single: jax.random.permutation(single, per_dev))(keys)
    return perms.reshape(-1).astype(jnp.int32)


def draw_pair_slots(key, part):
    ncols = ROW_TILES // TILES_DEV
    slot = jnp.arange(SLOTS, dtype=jnp.int32)
    device = slot // PAIRS_DEV
    within = slot % PAIRS_DEV
    row_index = device // ncols
    col_index = device % ncols
    first = jax.random.randint(jax.random.fold_in(key, 21), (SLOTS,), 0, ROW_TILES, dtype=jnp.int32)
    second = jax.random.randint(jax.random.fold_in(key, 22), (SLOTS,), 0, COL_TILES, dtype=jnp.int32)
    diagonal = within < TILES_DEV
    first = jnp.where(diagonal, col_index * TILES_DEV + within, first)
    second = jnp.where(diagonal, row_index * TILES_DEV + within, second)
    return jnp.stack([first, second]).astype(jnp.int32)


def draw_pair_count(key, part):
    base = jax.random.randint(jax.random.fold_in(key, 31), (GRID,), PAIRS_DEV // 4, PAIRS_DEV // 2 + 1, dtype=jnp.int32)
    dense = jax.random.randint(jax.random.fold_in(key, 32), (GRID,), 0, 8, dtype=jnp.int32) == 0
    chosen = jax.random.randint(jax.random.fold_in(key, 33), (), 0, GRID, dtype=jnp.int32)
    full = dense | (jnp.arange(GRID, dtype=jnp.int32) == chosen)
    return jnp.where(full, PAIRS_DEV, base).astype(jnp.int32)


def place_ends(result, key, low, largest):
    longest = result.shape.index(max(result.shape))
    spots = []
    for shift in (0, 1):
        where = [jax.random.randint(jax.random.fold_in(key, axis), (), 0, length) for axis, length in enumerate(result.shape)]
        where[longest] = (where[longest] + shift) % result.shape[longest]
        spots.append(tuple(where))
    return result.at[spots[0]].set(low).at[spots[1]].set(largest)


def block_scale(rng, extent, cuts, low, high):
    loudness, own = 1.0, jax.random.fold_in(rng, 6)
    for dim, shards_of in cuts:
        steps = jnp.exp(jax.random.uniform(jax.random.fold_in(own, dim), (shards_of,), jnp.float32, low / len(cuts), high / len(cuts)))
        loudness = loudness * jnp.repeat(steps, extent[dim] // shards_of).reshape([-1 if axis == dim else 1 for axis in range(len(extent))])
    return loudness


def bell_draw(stream_key, shape, width, bound, cuts=(), kind=jnp.bfloat16):
    gain = block_scale(stream_key, shape, cuts, -0.22, 0.18) if cuts else 1.0
    result = jax.random.normal(stream_key, shape, jnp.float32) * width * gain
    return jnp.minimum(jnp.maximum(result, -bound), bound).astype(kind)


def setup_inputs(seed: int = 0, part: int = 0) -> dict:
    arg_keys = jax.random.split(jax.random.key(seed), 8)
    part_keys = jax.random.split(jax.random.fold_in(arg_keys[7], part), 8)
    return {
        "positions": bell_draw(part_keys[0], (3, NPART), 1.0, 6.0, ((1, 16),), jnp.float32),
        "strengths": bell_draw(part_keys[1], (3, NPART), 1.0, 6.0, ((1, 16),), jnp.float32),
        "cores": jnp.clip(jnp.exp(math.log(1.0) - 1.2039728 * jax.random.uniform(part_keys[2], (NPART,), jnp.float32) ** block_scale(part_keys[2], (NPART,), ((0, 16),), -0.2, 0.2)), 0.3, 1.0),
        "order": draw_order(jax.random.fold_in(jax.random.fold_in(arg_keys[7], part), 71), part),
        "tile_counts": place_ends(jax.random.randint(part_keys[4], (TILES,), TILE // 4, TILE + 1), jax.random.fold_in(part_keys[4], 1), TILE // 4, TILE).astype(jnp.int32),
        "pair_slots": draw_pair_slots(jax.random.fold_in(jax.random.fold_in(arg_keys[7], part), 71), part),
        "pair_count": draw_pair_count(jax.random.fold_in(jax.random.fold_in(arg_keys[7], part), 71), part),
    }


biot_factor = -1.0 / (4.0 * math.pi)

def cross_product(left, right):
    return jnp.stack([left[1] * right[2] - left[2] * right[1], left[2] * right[0] - left[0] * right[2], left[0] * right[1] - left[1] * right[0]])

def pair_terms(target, source, weight_t, weight_r):
    target_pos = target[0:3, :, :, None]
    source_pos = source[0:3, :, None, :]
    target_str = target[3:6, :, :, None]
    source_str = source[3:6, :, None, :]
    offset = target_pos - source_pos
    sigma_sq = 0.5 * (target[6][:, :, None] ** 2 + source[6][:, None, :] ** 2)
    rho_sq = (offset[0] * offset[0] + offset[1] * offset[1] + offset[2] * offset[2]) / sigma_sq
    inverse = lax.rsqrt(rho_sq + 1.0)
    inverse_sq = inverse * inverse
    inverse_five = inverse_sq * inverse_sq * inverse
    core_cube = sigma_sq * jnp.sqrt(sigma_sq)
    smooth = (rho_sq + 2.5) * inverse_five / core_cube
    gradient = -3.0 * (rho_sq + 3.5) * inverse_five * inverse_sq / (core_cube * sigma_sq)
    cross_src = cross_product(offset, source_str)
    cross_tgt = cross_product(offset, target_str)
    along_tgt = lax.optimization_barrier(jnp.sum(target_str * offset, axis=0))
    along_src = lax.optimization_barrier(jnp.sum(source_str * offset, axis=0))
    smooth_t = smooth * weight_t[:, None, None]
    grad_t = gradient * weight_t[:, None, None]
    vel_target = biot_factor * lax.optimization_barrier(jnp.sum(smooth_t * cross_src, axis=-1))
    mix_target = lax.optimization_barrier(jnp.sum(smooth_t * source_str, axis=-1))
    str_target = biot_factor * (cross_product(target[3:6], mix_target) + lax.optimization_barrier(jnp.sum(grad_t * along_tgt * cross_src, axis=-1)))
    smooth_r = smooth * weight_r[:, None, None]
    grad_r = gradient * weight_r[:, None, None]
    vel_source = -biot_factor * lax.optimization_barrier(jnp.sum(smooth_r * cross_tgt, axis=-2))
    mix_source = lax.optimization_barrier(jnp.sum(smooth_r * target_str, axis=-2))
    str_source = biot_factor * (-cross_product(mix_source, source[3:6]) + lax.optimization_barrier(jnp.sum(grad_r * along_src * cross_tgt, axis=-2)))
    return (jnp.concatenate([vel_target, str_target], axis=0), jnp.concatenate([vel_source, str_source], axis=0))

def reference(positions, strengths, cores, order, tile_counts, pair_slots, pair_count):
    per_dev = TILES_DEV * TILE
    spots = jnp.arange(NPART, dtype=jnp.int32)
    index = order + spots // per_dev * per_dev
    live = (spots % TILE < tile_counts[spots // TILE]).astype(jnp.float32)
    packed = jnp.concatenate([positions[:, index], strengths[:, index] * live, cores[index][None, :]], axis=0)
    tiles = packed.reshape(7, TILES, TILE)
    slot = jnp.arange(SLOTS, dtype=jnp.int32)
    device = slot // PAIRS_DEV
    row_index = device // N_COL
    col_index = device % N_COL
    first = pair_slots[0]
    second = pair_slots[1]
    target_tile = row_index * ROW_TILES + first
    source_tile = (second // TILES_DEV * N_COL + col_index) * TILES_DEV + second % TILES_DEV
    alive = (slot % PAIRS_DEV < pair_count[device]).astype(jnp.float32)
    react = alive * (target_tile != source_tile).astype(jnp.float32)
    blocks = SLOTS // PAIR_BLOCK

    def step(total, items):
        tgt_idx, src_idx, weight_t, weight_r = items
        tgt_terms, src_terms = pair_terms(tiles[:, tgt_idx], tiles[:, src_idx], weight_t, weight_r)
        total = total.at[:, tgt_idx].add(tgt_terms)
        total = total.at[:, src_idx].add(src_terms)
        return (total, None)
    items = (target_tile.reshape(blocks, PAIR_BLOCK), source_tile.reshape(blocks, PAIR_BLOCK), alive.reshape(blocks, PAIR_BLOCK), react.reshape(blocks, PAIR_BLOCK))
    total, _ = lax.scan(step, jnp.zeros((6, TILES, TILE), jnp.float32), items)
    total = total.reshape(6, NPART) * live
    return (total[0:3], total[3:6])
```

```python
import functools
import math

import jax
import jax.numpy as jnp
from jax import lax
from jax.experimental import pallas as pl
from jax.experimental.pallas import tpu as pltpu
from jax.sharding import PartitionSpec as P

TILE = 128
MESH = pl.DeviceIdType.MESH
VMEM = pl.BlockSpec(memory_space=pltpu.VMEM)
SMEM = pl.BlockSpec(memory_space=pltpu.SMEM)
HBM = pl.BlockSpec(memory_space=pltpu.HBM)
UNROLL = 14
CHUNK = 16

biot_factor = -1.0 / (4.0 * math.pi)


def peers(nrows, ncols):
    return [("col", k) for k in range(1, ncols)] + [("row", k) for k in range(1, nrows)]


def greet(nrows, ncols):
    barrier = pltpu.get_barrier_semaphore()
    for axis, k in peers(nrows, ncols):
        size = ncols if axis == "col" else nrows
        other = lax.rem(lax.axis_index(axis) + k, size)
        pl.semaphore_signal(barrier, inc=1, device_id={axis: other}, device_id_type=MESH)
    return barrier


def split(value):
    high = value.astype(jnp.bfloat16)
    return high, (value - high.astype(jnp.float32)).astype(jnp.bfloat16)


def cross(left, right):
    return [left[(k + 1) % 3] * right[(k + 2) % 3] - left[(k + 2) % 3] * right[(k + 1) % 3] for k in range(3)]


def wake_kernel(nrows, ncols, tiles, count_in, counts_in, slots_in, pos_in, strg_in, cores_in, order_in,
                sums_out, slots, count, counts, slot_rows, pos, strg, cores, order, raw, row_blk, col_blk, spread, ones, stage, row_w, col_w, tgt_buf, src_buf,
                tgt_terms, src_terms, row_sum, col_sum, row_held, col_held, load, send, recv):
    barrier = greet(nrows, ncols)
    pairs_in = [(pos_in, pos), (strg_in, strg), (cores_in, cores), (order_in, order), (counts_in, counts),
                (slots_in, slot_rows), (slots_in, slots), (count_in, count)]
    loads = [pltpu.make_async_copy(src, dst, load.at[n]) for n, (src, dst) in enumerate(pairs_in)]
    for copy in loads:
        copy.start()
    row = lax.axis_index("row")
    col = lax.axis_index("col")
    num_slots = slot_rows.shape[1]
    lane = lax.broadcasted_iota(jnp.int32, (8, TILE), 1)
    sub = lax.broadcasted_iota(jnp.int32, (8, TILE), 0)
    own_row = pl.multiple_of(col * tiles, tiles)
    own_col = pl.multiple_of(row * tiles, tiles)

    stage[...] = jnp.zeros_like(stage)
    rank = lax.broadcasted_iota(jnp.int32, (16, TILE), 0)
    for k in range(3):
        ones[:, k * TILE : (k + 1) * TILE] = jnp.where((rank == k) | (rank == 6 + k), 1.0, 0.0).astype(jnp.bfloat16)
    ones[:, 3 * TILE :] = jnp.where((rank > 11) & (rank < 15), 1.0, 0.0).astype(jnp.bfloat16)
    for copy in loads:
        copy.wait()
    for t in range(tiles):
        part = slice(t * TILE, (t + 1) * TILE)
        raw[t, 0:3, :] = pos[:, part]
        raw[t, 3:6, :] = strg[:, part]
        raw[t, 6:7, :] = cores[t : t + 1, :]
        raw[t, 7:8, :] = cores[t : t + 1, :]
    for t in range(tiles):
        spot = jnp.broadcast_to(order[t : t + 1, :], (8, TILE))
        inner = spot & (TILE - 1)
        outer = spot >> 7
        found = jnp.zeros((8, TILE), jnp.float32)
        for s in range(tiles):
            found = jnp.where(outer == s, jnp.take_along_axis(raw[s], inner, axis=1), found)
        keep = (lane < counts[t]) | (sub < 3) | (sub > 5)
        found = jnp.where(keep, found, 0.0)
        row_blk[own_row + t] = found
        col_blk[own_col + t] = found

    pl.semaphore_wait(barrier, nrows + ncols - 2)
    copies = []
    for n, (axis, k) in enumerate(peers(nrows, ncols)):
        size, me, block, at = (ncols, col, row_blk, own_row) if axis == "col" else (nrows, row, col_blk, own_col)
        copy = pltpu.make_async_remote_copy(
            src_ref=block.at[pl.ds(at, tiles)],
            dst_ref=block.at[pl.ds(at, tiles)],
            send_sem=send.at[0, n],
            recv_sem=recv.at[0, n],
            device_id={axis: lax.rem(me + k, size)},
            device_id_type=MESH,
        )
        copy.start()
        copies.append(copy)

    def weights(block, at, out):
        some = block.at[pl.ds(at, tiles)]
        x = [some[:, k, :] for k in range(3)]
        a = [some[:, 3 + k, :] for k in range(3)]
        for k, value in enumerate(a + cross(x, a)):
            high = value.astype(jnp.bfloat16).astype(jnp.float32)
            stage[:, k, :] = high
            stage[:, 6 + k, :] = value - high
        sigma = some[:, 6, :]
        rest = 0.5 * sigma * sigma
        for k in range(3):
            high = rest.astype(jnp.bfloat16).astype(jnp.float32)
            stage[:, 12 + k, :] = high
            rest = rest - high
        for t in range(tiles):
            both = stage[t].astype(jnp.bfloat16)
            out[at + t, :, 0:TILE] = both
            out[at + t, :, TILE:] = both

    def prepare_row(k):
        at = pl.multiple_of(lax.rem(col + ncols - k, ncols) * tiles, tiles)
        weights(row_blk, at, row_w)
        for t in range(tiles):
            column = row_blk[at + t].T
            for j in range(3):
                spread[at + t, j] = jnp.broadcast_to(column[:, j : j + 1], (TILE, TILE))
            rest = lax.dot_general(row_w[at + t, :, 0:TILE], ones[...], (((0,), (0,)), ((), ())),
                                   preferred_element_type=jnp.float32)
            for j in range(4):
                spread[at + t, 3 + j] = rest[:, j * TILE : (j + 1) * TILE]

    def prepare_col(k):
        weights(col_blk, pl.multiple_of(lax.rem(row + nrows - k, nrows) * tiles, tiles), col_w)

    def pair(u, s, ti, sj, react):
        src = col_blk[sj]
        xj = [src[k : k + 1, :] for k in range(7)]
        hj = 0.5 * xj[6] * xj[6]
        for c in range(TILE // CHUNK):
            at = slice(c * CHUNK, (c + 1) * CHUNK)
            at2 = slice(TILE + c * CHUNK, TILE + (c + 1) * CHUNK)
            xi = [spread[ti, k, at, :] for k in range(7)]
            dx = xi[0] - xj[0]
            dy = xi[1] - xj[1]
            dz = xi[2] - xj[2]
            s2 = xi[6] + hj
            d = dx * dx + dy * dy + dz * dz + s2
            inv = lax.rsqrt(d)
            inv2 = inv * inv
            inv3 = inv2 * inv
            w = s2 * (inv3 * inv2)
            q = inv3 + 1.5 * w
            f = (q + w) * inv2
            g = f * (xi[3] * dx + xi[4] * dy + xi[5] * dz)
            q1, q2 = split(q)
            g1, g2 = split(g)
            tgt_buf[u, at, 0:TILE] = q1
            tgt_buf[u, at, TILE:] = q2
            tgt_buf[u, at2, 0:TILE] = g1
            tgt_buf[u, at2, TILE:] = g2
            if react:
                h = f * (xj[3] * dx + xj[4] * dy + xj[5] * dz)
                h1, h2 = split(h)
                src_buf[u, at, 0:TILE] = q1
                src_buf[u, at, TILE:] = h1
                src_buf[u, at2, 0:TILE] = q2
                src_buf[u, at2, TILE:] = h2
        out = lax.dot_general(col_w[sj], tgt_buf[u], (((1,), (1,)), ((), ())), preferred_element_type=jnp.float32)
        tgt_terms[s, 0:6, :] = out[0:6] + out[6:12]
        if react:
            out = lax.dot_general(row_w[ti], src_buf[u], (((1,), (0,)), ((), ())), preferred_element_type=jnp.float32)
            src_terms[s, 0:6, :] = out[0:6] + out[6:12]

    prepare_row(0)
    prepare_col(0)
    src_terms[0:tiles] = jnp.zeros((tiles, 8, 2 * TILE), jnp.float32)

    def diagonal(step, _):
        for u in range(4):
            t = step * 4 + u
            pair(u, t, own_row + t, own_col + t, False)
        return 0

    lax.fori_loop(0, tiles // 4, diagonal, 0)

    def arrived(axis, size, me, block, base, prepare):
        def step(k, _):
            other = lax.rem(me + size - k, size)
            place = block.at[pl.ds(pl.multiple_of(other * tiles, tiles), tiles)]
            pltpu.make_async_remote_copy(
                src_ref=place,
                dst_ref=place,
                send_sem=send.at[0, base + k - 1],
                recv_sem=recv.at[0, base + k - 1],
                device_id={axis: other},
                device_id_type=MESH,
            ).wait_recv()
            prepare(k)
            return 0

        lax.fori_loop(1, size, step, 0)

    arrived("col", ncols, col, row_blk, 0, prepare_row)
    arrived("row", nrows, row, col_blk, ncols - 1, prepare_col)

    def visit(step, _):
        for u in range(UNROLL):
            s = tiles + step * UNROLL + u
            pair(u, s, slots[0, s], slots[1, s], True)
        return 0

    lax.fori_loop(0, (num_slots - tiles) // UNROLL, visit, 0)

    first = slot_rows[0:1, :]
    second = slot_rows[1:2, :]
    slot = lax.broadcasted_iota(jnp.int32, (1, num_slots), 1)
    first = jnp.where(slot < tiles, own_row + slot, first)
    gi = row * (ncols * tiles) + first
    gj = ((second // tiles) * ncols + col) * tiles + second % tiles
    alive = slot < count[0]
    row_sel = jnp.where(alive, first, -1)
    col_sel = jnp.where(alive & (gi != gj) & (slot >= tiles), second, -1)

    def finish(select, terms, block, out, sign):
        size = block.shape[0]
        here = lax.broadcasted_iota(jnp.int32, (size, num_slots), 0)
        hot = jnp.where(here == select, 1.0, 0.0).astype(jnp.bfloat16)
        qs, fs = [], []
        for k in range(6):
            high, low = split(terms[:, k, :])
            value = jnp.dot(hot, high, preferred_element_type=jnp.float32)
            value += jnp.dot(hot, low, preferred_element_type=jnp.float32)
            qs.append(value[:, 0:TILE])
            fs.append(value[:, TILE:])
        x = [block[:, k, :] for k in range(3)]
        a = [block[:, 3 + k, :] for k in range(3)]
        velocity = cross(x, qs[0:3])
        turn = cross(a, qs[0:3])
        steep = cross(x, fs[0:3])
        for k in range(3):
            v = biot_factor * (velocity[k] - qs[3 + k])
            w = biot_factor * (turn[k] - (3.0 * sign) * (steep[k] - fs[3 + k]))
            out[:, k] = v.reshape(size // tiles, tiles, TILE)
            out[:, 3 + k] = w.reshape(size // tiles, tiles, TILE)

    for copy in copies:
        copy.wait_send()

    def send_all(axis, first_sem, size, me, sums, held):
        started = []
        for k in range(1, size):
            other = lax.rem(me + k, size)
            copy = pltpu.make_async_remote_copy(
                src_ref=sums.at[other],
                dst_ref=held.at[k - 1],
                send_sem=send.at[1, first_sem + k - 1],
                recv_sem=recv.at[1, first_sem + k - 1],
                device_id={axis: other},
                device_id_type=MESH,
            )
            copy.start()
            started.append((copy, held.at[k - 1]))
        return started

    finish(row_sel, tgt_terms, row_blk, row_sum, 1.0)
    started = send_all("col", 0, ncols, col, row_sum, row_held)
    finish(col_sel, src_terms, col_blk, col_sum, -1.0)
    started += send_all("row", ncols - 1, nrows, row, col_sum, col_held)
    total = row_sum[col] + col_sum[row]
    for copy, held in started:
        copy.wait_recv()
        total = total + held[...]
    for t in range(tiles):
        part = slice(t * TILE, (t + 1) * TILE)
        live = lane[0:1, :] < counts[t]
        for k in range(3):
            sums_out[k : k + 1, part] = jnp.where(live, total[k, t : t + 1, :], 0.0)
            sums_out[3 + k : 4 + k, part] = jnp.where(live, total[3 + k, t : t + 1, :], 0.0)
    for copy, _ in started:
        copy.wait_send()


def shards(nrows, ncols, positions, strengths, cores, order, tile_counts, pair_slots, pair_count):
    tiles = tile_counts.shape[0]
    num_slots = pair_slots.shape[1]
    others = nrows + ncols - 2
    nt, ns = ncols * tiles, nrows * tiles
    f32, bf16 = jnp.float32, jnp.bfloat16
    sums = pl.pallas_call(
        functools.partial(wake_kernel, nrows, ncols, tiles),
        out_shape=pltpu.VMEM((6, tiles * TILE), f32),
        in_specs=[HBM] * 7,
        out_specs=VMEM,
        scratch_shapes=[
            pltpu.SMEM((2, num_slots), jnp.int32),
            pltpu.SMEM((1,), jnp.int32),
            pltpu.SMEM((tiles,), jnp.int32),
            pltpu.VMEM((2, num_slots), jnp.int32),
            pltpu.VMEM((3, tiles * TILE), f32),
            pltpu.VMEM((3, tiles * TILE), f32),
            pltpu.VMEM((tiles, TILE), f32),
            pltpu.VMEM((tiles, TILE), jnp.int32),
            pltpu.VMEM((tiles, 8, TILE), f32),
            pltpu.VMEM((nt, 8, TILE), f32),
            pltpu.VMEM((ns, 8, TILE), f32),
            pltpu.VMEM((nt, 7, TILE, TILE), f32),
            pltpu.VMEM((16, 4 * TILE), bf16),
            pltpu.VMEM((tiles, 16, TILE), f32),
            pltpu.VMEM((nt, 16, 2 * TILE), bf16),
            pltpu.VMEM((ns, 16, 2 * TILE), bf16),
            pltpu.VMEM((UNROLL, 2 * TILE, 2 * TILE), bf16),
            pltpu.VMEM((UNROLL, 2 * TILE, 2 * TILE), bf16),
            pltpu.VMEM((num_slots, 8, 2 * TILE), f32),
            pltpu.VMEM((num_slots, 8, 2 * TILE), f32),
            pltpu.VMEM((ncols, 6, tiles, TILE), f32),
            pltpu.VMEM((nrows, 6, tiles, TILE), f32),
            pltpu.VMEM((ncols - 1, 6, tiles, TILE), f32),
            pltpu.VMEM((nrows - 1, 6, tiles, TILE), f32),
            pltpu.SemaphoreType.DMA((8,)),
            pltpu.SemaphoreType.DMA((2, others)),
            pltpu.SemaphoreType.DMA((2, others)),
        ],
        compiler_params=pltpu.CompilerParams(
            collective_id=0, has_side_effects=True, vmem_limit_bytes=56 * 1024 * 1024
        ),
        name="wake",
    )(pair_count, tile_counts, pair_slots, positions, strengths,
      cores.reshape(tiles, TILE), order.reshape(tiles, TILE))
    return sums[0:3], sums[3:6]


def solution(mesh):
    whole = ("groups", "row", "col")
    in_specs = (P(None, whole), P(None, whole), P(whole), P(whole), P(whole), P(None, whole), P(whole))
    out_specs = (P(None, whole), P(None, whole))
    body = functools.partial(shards, mesh.shape["row"], mesh.shape["col"])
    return jax.shard_map(body, mesh=mesh, in_specs=in_specs, out_specs=out_specs, check_vma=False)
```

```python
import functools
import math

import jax
import jax.numpy as jnp
from jax import lax
from jax.experimental import pallas as pl
from jax.experimental.pallas import tpu as pltpu
from jax.sharding import PartitionSpec as P

TILE = 128
MESH = pl.DeviceIdType.MESH
VMEM = pl.BlockSpec(memory_space=pltpu.VMEM)
SMEM = pl.BlockSpec(memory_space=pltpu.SMEM)
HBM = pl.BlockSpec(memory_space=pltpu.HBM)
UNROLL = 14
CHUNK = 16
MOMENTS = 24
WROWS = 80
FROWS = 32
PLANES = 32

biot_factor = -1.0 / (4.0 * math.pi)


def peers(nrows, ncols):
    return [("col", k) for k in range(1, ncols)] + [("row", k) for k in range(1, nrows)]


def greet(nrows, ncols):
    barrier = pltpu.get_barrier_semaphore()
    for axis, k in peers(nrows, ncols):
        size = ncols if axis == "col" else nrows
        other = lax.rem(lax.axis_index(axis) + k, size)
        pl.semaphore_signal(barrier, inc=1, device_id={axis: other}, device_id_type=MESH)
    return barrier


def split(value):
    high = value.astype(jnp.bfloat16)
    return high, (value - high.astype(jnp.float32)).astype(jnp.bfloat16)


def thirds(value):
    first = value.astype(jnp.bfloat16).astype(jnp.float32)
    rest = value - first
    second = rest.astype(jnp.bfloat16).astype(jnp.float32)
    return first, second, rest - second


def cross(left, right):
    return [left[(k + 1) % 3] * right[(k + 2) % 3] - left[(k + 2) % 3] * right[(k + 1) % 3] for k in range(3)]


def dot3(left, right):
    return left[0] * right[0] + left[1] * right[1] + left[2] * right[2]


def wake_kernel(nrows, ncols, tiles, count_in, counts_in, slots_in, pos_in, strg_in, cores_in, order_in,
                sums_out, slots, count, counts, slot_rows, pos, strg, cores, order, raw, row_blk, col_blk, center,
                stage, row_near, col_near, col_wide, row_w, col_w, row_f, col_f, near_buf, tgt_buf, src_buf,
                tgt_terms, src_terms, row_sum, col_sum, row_held, col_held, load, send, recv):
    barrier = greet(nrows, ncols)
    pairs_in = [(pos_in, pos), (strg_in, strg), (cores_in, cores), (order_in, order), (counts_in, counts),
                (slots_in, slot_rows), (slots_in, slots), (count_in, count)]
    loads = [pltpu.make_async_copy(src, dst, load.at[n]) for n, (src, dst) in enumerate(pairs_in)]
    for copy in loads:
        copy.start()
    row = lax.axis_index("row")
    col = lax.axis_index("col")
    num_slots = slot_rows.shape[1]
    lane = lax.broadcasted_iota(jnp.int32, (8, TILE), 1)
    sub = lax.broadcasted_iota(jnp.int32, (8, TILE), 0)

    for copy in loads:
        copy.wait()
    for t in range(tiles):
        part = slice(t * TILE, (t + 1) * TILE)
        raw[t, 0:3, :] = pos[:, part]
        raw[t, 3:6, :] = strg[:, part]
        raw[t, 6:7, :] = cores[t : t + 1, :]
        raw[t, 7:8, :] = cores[t : t + 1, :]
    for t in range(tiles):
        spot = jnp.broadcast_to(order[t : t + 1, :], (8, TILE))
        inner = spot & (TILE - 1)
        outer = spot >> 7
        found = jnp.zeros((8, TILE), jnp.float32)
        for s in range(tiles):
            found = jnp.where(outer == s, jnp.take_along_axis(raw[s], inner, axis=1), found)
        keep = (lane < counts[t]) | (sub < 3) | (sub > 5)
        found = jnp.where(keep, found, 0.0)
        own = pl.ds(t, 7, stride=tiles)
        row_blk[col, own, :] = found[0:7]
        col_blk[row, own, :] = found[0:7]

    pl.semaphore_wait(barrier, nrows + ncols - 2)
    copies = []
    for n, (axis, k) in enumerate(peers(nrows, ncols)):
        size, me, block = (ncols, col, row_blk) if axis == "col" else (nrows, row, col_blk)
        copy = pltpu.make_async_remote_copy(
            src_ref=block.at[me],
            dst_ref=block.at[me],
            send_sem=send.at[0, n],
            recv_sem=recv.at[0, n],
            device_id={axis: lax.rem(me + k, size)},
            device_id_type=MESH,
        )
        copy.start()
        copies.append(copy)

    for t in range(tiles):
        stage[t * WROWS + 3 * MOMENTS : (t + 1) * WROWS, :] = jnp.zeros((WROWS - 3 * MOMENTS, TILE), jnp.float32)
    rank = lax.rem(lax.broadcasted_iota(jnp.int32, (tiles * FROWS, TILE), 0), FROWS)
    row_near[...] = jnp.where((rank > 20) & (rank < 24), 1.0, 0.0)
    col_near[...] = jnp.where((rank > 17) & (rank < 21), 1.0, 0.0)
    col_wide[...] = jnp.where((rank > 23) & (rank < 27), 1.0, 0.0)
    for plane in range(PLANES):
        src_terms[plane * num_slots : plane * num_slots + tiles, :] = jnp.zeros((tiles, TILE), jnp.float32)
    for k in range(3):
        mean = jnp.sum(row_blk[col, k * tiles : (k + 1) * tiles], keepdims=True) * (1.0 / (tiles * TILE))
        center[k] = jnp.broadcast_to(mean, (tiles, TILE))

    def part(block, at, k):
        return block[at, k * tiles : (k + 1) * tiles]

    def put(out, rows, r, value):
        out[pl.ds(r, tiles, stride=rows), :] = value

    def prepare(block, at, weights, near, wide_near, features, target):
        x = [part(block, at, k) - center[k] for k in range(3)]
        a = [part(block, at, 3 + k) for k in range(3)]
        b = cross(x, a)
        moments = a + b + [p * v for p in x for v in a] + [p * v for p in x for v in b]
        for r, value in enumerate(moments):
            for j, piece in enumerate(thirds(value)):
                put(stage, WROWS, j * MOMENTS + r, piece)
        sigma = part(block, at, 6)
        half = 0.5 * sigma * sigma
        norm = thirds(dot3(x, x) + half)
        wide = thirds(1.5 * half)
        places = [thirds(value if target else -2.0 * value) for value in x]
        for n, j in enumerate((0, 0, 0, 1, 1, 2) if target else (0, 1, 2, 0, 1, 0)):
            for k in range(3):
                put(near, FROWS, 3 * n + k, places[k][j])
        for j in range(3):
            put(near, FROWS, (18 if target else 21) + j, norm[j])
            put(wide_near, FROWS, (24 if target else 21) + j, wide[j])
        for t in range(tiles):
            weights[at * tiles + t] = stage[t * WROWS : (t + 1) * WROWS, :].astype(jnp.bfloat16)
            some = slice(t * FROWS, (t + 1) * FROWS)
            features[at * tiles + t, :, 0:TILE] = near[some, :].astype(jnp.bfloat16)
            if not target:
                features[at * tiles + t, :, TILE:] = wide_near[some, :].astype(jnp.bfloat16)

    def prepare_row(k):
        prepare(row_blk, lax.rem(col + ncols - k, ncols), row_w, row_near, row_near, row_f, True)

    def prepare_col(k):
        prepare(col_blk, lax.rem(row + nrows - k, nrows), col_w, col_near, col_wide, col_f, False)

    def keep_terms(terms, s, out):
        for n, (first, at) in enumerate(((0, 0), (0, TILE), (8, TILE), (16, TILE))):
            total = out[first : first + 8, at : at + TILE]
            for j in (1, 2):
                total = total + out[j * MOMENTS + first : j * MOMENTS + first + 8, at : at + TILE]
            terms[pl.ds(n * 8 * num_slots + s, 8, stride=num_slots), :] = total

    def meet(u, ti, sj):
        near_buf[u] = lax.dot_general(row_f[ti], col_f[sj], (((0,), (0,)), ((), ())), preferred_element_type=jnp.float32)

    def spread(u, react):
        near = near_buf[u]
        for c in range(TILE // CHUNK):
            at = slice(c * CHUNK, (c + 1) * CHUNK)
            at2 = slice(TILE + c * CHUNK, TILE + (c + 1) * CHUNK)
            inv = lax.rsqrt(near[at, 0:TILE])
            inv2 = inv * inv
            ratio = near[at, TILE:] * inv2
            inv3 = inv2 * inv
            q1, q2 = split(inv3 * (ratio + 1.0))
            f1, f2 = split((inv3 * inv2) * (ratio + 0.6))
            tgt_buf[u, at, 0:TILE] = q1
            tgt_buf[u, at, TILE:] = q2
            tgt_buf[u, at2, 0:TILE] = f1
            tgt_buf[u, at2, TILE:] = f2
            if react:
                src_buf[u, at, 0:TILE] = q1
                src_buf[u, at, TILE:] = f1
                src_buf[u, at2, 0:TILE] = q2
                src_buf[u, at2, TILE:] = f2

    def gather(u, s, ti, sj, react):
        some = col_w[sj]
        both = jnp.concatenate([some, some], axis=1)
        out = lax.dot_general(both, tgt_buf[u], (((1,), (1,)), ((), ())), preferred_element_type=jnp.float32)
        keep_terms(tgt_terms, s, out)
        if react:
            some = row_w[ti]
            both = jnp.concatenate([some, some], axis=1)
            out = lax.dot_general(both, src_buf[u], (((1,), (0,)), ((), ())), preferred_element_type=jnp.float32)
            keep_terms(src_terms, s, out)

    def group(places, react):
        for u, (s, ti, sj) in enumerate(places):
            meet(u, ti, sj)
        for u, (s, ti, sj) in enumerate(places):
            spread(u, react)
        for u, (s, ti, sj) in enumerate(places):
            gather(u, s, ti, sj, react)

    prepare_row(0)
    prepare_col(0)

    def diagonal(step, _):
        places = [(step * 4 + u, col * tiles + step * 4 + u, row * tiles + step * 4 + u) for u in range(4)]
        group(places, False)
        return 0

    lax.fori_loop(0, tiles // 4, diagonal, 0)

    def arrived(axis, size, me, block, base, prepare_one):
        def step(k, _):
            other = lax.rem(me + size - k, size)
            place = block.at[other]
            pltpu.make_async_remote_copy(
                src_ref=place,
                dst_ref=place,
                send_sem=send.at[0, base + k - 1],
                recv_sem=recv.at[0, base + k - 1],
                device_id={axis: other},
                device_id_type=MESH,
            ).wait_recv()
            prepare_one(k)
            return 0

        lax.fori_loop(1, size, step, 0)

    arrived("col", ncols, col, row_blk, 0, prepare_row)
    arrived("row", nrows, row, col_blk, ncols - 1, prepare_col)

    def visit(step, _):
        first = tiles + step * UNROLL
        group([(first + u, slots[0, first + u], slots[1, first + u]) for u in range(UNROLL)], True)
        return 0

    lax.fori_loop(0, (num_slots - tiles) // UNROLL, visit, 0)

    first = slot_rows[0:1, :]
    second = slot_rows[1:2, :]
    slot = lax.broadcasted_iota(jnp.int32, (1, num_slots), 1)
    first = jnp.where(slot < tiles, col * tiles + slot, first)
    gi = row * (ncols * tiles) + first
    gj = ((second // tiles) * ncols + col) * tiles + second % tiles
    alive = slot < count[0]
    row_sel = jnp.where(alive, first, -1)
    col_sel = jnp.where(alive & (gi != gj) & (slot >= tiles), second, -1)

    def finish(select, terms, block, out):
        size = block.shape[0] * tiles
        here = lax.broadcasted_iota(jnp.int32, (size, num_slots), 0)
        hot = jnp.where(here == select, 1.0, 0.0)
        hot = jnp.concatenate([hot, hot, hot], axis=1).astype(jnp.bfloat16)
        sums = []
        for n in range(PLANES // 2):
            pieces = [thirds(terms[(2 * n + m) * num_slots : (2 * n + m + 1) * num_slots, :]) for m in range(2)]
            rows = jnp.concatenate([jnp.concatenate([pieces[0][j], pieces[1][j]], axis=1) for j in range(3)], axis=0)
            value = jnp.dot(hot, rows.astype(jnp.bfloat16), preferred_element_type=jnp.float32)
            sums += [value[:, 0:TILE], value[:, TILE:]]
        qa, qb, fa, fb = sums[0:3], sums[3:6], sums[8:11], sums[11:14]
        fxa, fxb = sums[14:23], sums[23:32]
        x = [block[:, k * tiles : (k + 1) * tiles].reshape(size, TILE) - center[k, 0:1] for k in range(3)]
        a = [block[:, (3 + k) * tiles : (4 + k) * tiles].reshape(size, TILE) for k in range(3)]
        velocity = cross(x, qa)
        turn = cross(a, qa)
        along = dot3(a, x)
        spin = cross(x, fa)
        toward = [dot3(a, [fxa[3 * k + m] for k in range(3)]) for m in range(3)]
        swing = cross(x, toward)
        for k in range(3):
            steep = along * (spin[k] - fb[k]) - swing[k] + dot3(a, [fxb[3 * m + k] for m in range(3)])
            v = biot_factor * (velocity[k] - qb[k])
            w = biot_factor * (turn[k] - 5.0 * steep)
            out[:, k] = v.reshape(size // tiles, tiles, TILE)
            out[:, 3 + k] = w.reshape(size // tiles, tiles, TILE)

    for copy in copies:
        copy.wait_send()

    def send_all(axis, first_sem, size, me, sums, held):
        started = []
        for k in range(1, size):
            other = lax.rem(me + k, size)
            copy = pltpu.make_async_remote_copy(
                src_ref=sums.at[other],
                dst_ref=held.at[k - 1],
                send_sem=send.at[1, first_sem + k - 1],
                recv_sem=recv.at[1, first_sem + k - 1],
                device_id={axis: other},
                device_id_type=MESH,
            )
            copy.start()
            started.append((copy, held.at[k - 1]))
        return started

    finish(row_sel, tgt_terms, row_blk, row_sum)
    started = send_all("col", 0, ncols, col, row_sum, row_held)
    finish(col_sel, src_terms, col_blk, col_sum)
    started += send_all("row", ncols - 1, nrows, row, col_sum, col_held)
    total = row_sum[col] + col_sum[row]
    for copy, held in started:
        copy.wait_recv()
        total = total + held[...]
    for t in range(tiles):
        part = slice(t * TILE, (t + 1) * TILE)
        live = lane[0:1, :] < counts[t]
        for k in range(3):
            sums_out[k : k + 1, part] = jnp.where(live, total[k, t : t + 1, :], 0.0)
            sums_out[3 + k : 4 + k, part] = jnp.where(live, total[3 + k, t : t + 1, :], 0.0)
    for copy, _ in started:
        copy.wait_send()


def shards(nrows, ncols, positions, strengths, cores, order, tile_counts, pair_slots, pair_count):
    tiles = tile_counts.shape[0]
    num_slots = pair_slots.shape[1]
    others = nrows + ncols - 2
    nt, ns = ncols * tiles, nrows * tiles
    f32, bf16 = jnp.float32, jnp.bfloat16
    sums = pl.pallas_call(
        functools.partial(wake_kernel, nrows, ncols, tiles),
        out_shape=pltpu.VMEM((6, tiles * TILE), f32),
        in_specs=[HBM] * 7,
        out_specs=VMEM,
        scratch_shapes=[
            pltpu.SMEM((2, num_slots), jnp.int32),
            pltpu.SMEM((1,), jnp.int32),
            pltpu.SMEM((tiles,), jnp.int32),
            pltpu.VMEM((2, num_slots), jnp.int32),
            pltpu.VMEM((3, tiles * TILE), f32),
            pltpu.VMEM((3, tiles * TILE), f32),
            pltpu.VMEM((tiles, TILE), f32),
            pltpu.VMEM((tiles, TILE), jnp.int32),
            pltpu.VMEM((tiles, 8, TILE), f32),
            pltpu.VMEM((ncols, 7 * tiles, TILE), f32),
            pltpu.VMEM((nrows, 7 * tiles, TILE), f32),
            pltpu.VMEM((3, tiles, TILE), f32),
            pltpu.VMEM((tiles * WROWS, TILE), f32),
            pltpu.VMEM((tiles * FROWS, TILE), f32),
            pltpu.VMEM((tiles * FROWS, TILE), f32),
            pltpu.VMEM((tiles * FROWS, TILE), f32),
            pltpu.VMEM((nt, WROWS, TILE), bf16),
            pltpu.VMEM((ns, WROWS, TILE), bf16),
            pltpu.VMEM((nt, FROWS, TILE), bf16),
            pltpu.VMEM((ns, FROWS, 2 * TILE), bf16),
            pltpu.VMEM((UNROLL, TILE, 2 * TILE), f32),
            pltpu.VMEM((UNROLL, 2 * TILE, 2 * TILE), bf16),
            pltpu.VMEM((UNROLL, 2 * TILE, 2 * TILE), bf16),
            pltpu.VMEM((PLANES * num_slots, TILE), f32),
            pltpu.VMEM((PLANES * num_slots, TILE), f32),
            pltpu.VMEM((ncols, 6, tiles, TILE), f32),
            pltpu.VMEM((nrows, 6, tiles, TILE), f32),
            pltpu.VMEM((ncols - 1, 6, tiles, TILE), f32),
            pltpu.VMEM((nrows - 1, 6, tiles, TILE), f32),
            pltpu.SemaphoreType.DMA((8,)),
            pltpu.SemaphoreType.DMA((2, others)),
            pltpu.SemaphoreType.DMA((2, others)),
        ],
        compiler_params=pltpu.CompilerParams(
            collective_id=0, has_side_effects=True, vmem_limit_bytes=56 * 1024 * 1024
        ),
        name="wake",
    )(pair_count, tile_counts, pair_slots, positions, strengths,
      cores.reshape(tiles, TILE), order.reshape(tiles, TILE))
    return sums[0:3], sums[3:6]


def solution(mesh):
    whole = ("groups", "row", "col")
    in_specs = (P(None, whole), P(None, whole), P(whole), P(whole), P(whole), P(None, whole), P(whole))
    out_specs = (P(None, whole), P(None, whole))
    body = functools.partial(shards, mesh.shape["row"], mesh.shape["col"])
    return jax.shard_map(body, mesh=mesh, in_specs=in_specs, out_specs=out_specs, check_vma=False)
```

```python
import functools
import math

import jax
import jax.numpy as jnp
from jax import lax
from jax.experimental import pallas as pl
from jax.experimental.pallas import tpu as pltpu
from jax.sharding import PartitionSpec as P

TILE = 128
MESH = pl.DeviceIdType.MESH
VMEM = pl.BlockSpec(memory_space=pltpu.VMEM)
SMEM = pl.BlockSpec(memory_space=pltpu.SMEM)
HBM = pl.BlockSpec(memory_space=pltpu.HBM)
UNROLL = 14
CHUNK = 16
MOMENTS = 24
WROWS = 80
WPITCH = 84
FROWS = 32
FPITCH = 36
PLANES = 32

biot_factor = -1.0 / (4.0 * math.pi)


def peers(nrows, ncols):
    return [("col", k) for k in range(1, ncols)] + [("row", k) for k in range(1, nrows)]


def greet(nrows, ncols):
    barrier = pltpu.get_barrier_semaphore()
    for axis, k in peers(nrows, ncols):
        size = ncols if axis == "col" else nrows
        other = lax.rem(lax.axis_index(axis) + k, size)
        pl.semaphore_signal(barrier, inc=1, device_id={axis: other}, device_id_type=MESH)
    return barrier


def split(value):
    high = value.astype(jnp.bfloat16)
    return high, (value - high.astype(jnp.float32)).astype(jnp.bfloat16)


def thirds(value):
    first = value.astype(jnp.bfloat16).astype(jnp.float32)
    rest = value - first
    second = rest.astype(jnp.bfloat16).astype(jnp.float32)
    return first, second, rest - second


def cross(left, right):
    return [left[(k + 1) % 3] * right[(k + 2) % 3] - left[(k + 2) % 3] * right[(k + 1) % 3] for k in range(3)]


def dot3(left, right):
    return left[0] * right[0] + left[1] * right[1] + left[2] * right[2]


def wake_kernel(nrows, ncols, tiles, count_in, counts_in, slots_in, pos_in, strg_in, cores_in, order_in,
                sums_out, slots, count, counts, slot_rows, pos, strg, cores, order, raw, row_blk, col_blk, center,
                stage, row_near, col_near, col_wide, row_w, col_w, row_f, col_f, near_buf, tgt_buf, src_buf,
                tgt_terms, src_terms, row_sum, col_sum, row_held, col_held, load, send, recv):
    barrier = greet(nrows, ncols)
    pairs_in = [(pos_in, pos), (strg_in, strg), (cores_in, cores), (order_in, order), (counts_in, counts),
                (slots_in, slot_rows), (slots_in, slots), (count_in, count)]
    loads = [pltpu.make_async_copy(src, dst, load.at[n]) for n, (src, dst) in enumerate(pairs_in)]
    for copy in loads:
        copy.start()
    row = lax.axis_index("row")
    col = lax.axis_index("col")
    num_slots = slot_rows.shape[1]
    pitch = num_slots + 4
    lane = lax.broadcasted_iota(jnp.int32, (8, TILE), 1)
    sub = lax.broadcasted_iota(jnp.int32, (8, TILE), 0)

    for copy in loads:
        copy.wait()
    for t in range(tiles):
        part = slice(t * TILE, (t + 1) * TILE)
        raw[t, 0:3, :] = pos[:, part]
        raw[t, 3:6, :] = strg[:, part]
        raw[t, 6:7, :] = cores[t : t + 1, :]
        raw[t, 7:8, :] = cores[t : t + 1, :]
    for t in range(tiles):
        spot = jnp.broadcast_to(order[t : t + 1, :], (8, TILE))
        inner = spot & (TILE - 1)
        outer = spot >> 7
        found = jnp.zeros((8, TILE), jnp.float32)
        for s in range(tiles):
            found = jnp.where(outer == s, jnp.take_along_axis(raw[s], inner, axis=1), found)
        keep = (lane < counts[t]) | (sub < 3) | (sub > 5)
        found = jnp.where(keep, found, 0.0)
        own = pl.ds(t, 7, stride=tiles)
        row_blk[col, own, :] = found[0:7]
        col_blk[row, own, :] = found[0:7]

    pl.semaphore_wait(barrier, nrows + ncols - 2)
    copies = []
    for n, (axis, k) in enumerate(peers(nrows, ncols)):
        size, me, block = (ncols, col, row_blk) if axis == "col" else (nrows, row, col_blk)
        copy = pltpu.make_async_remote_copy(
            src_ref=block.at[me],
            dst_ref=block.at[me],
            send_sem=send.at[0, n],
            recv_sem=recv.at[0, n],
            device_id={axis: lax.rem(me + k, size)},
            device_id_type=MESH,
        )
        copy.start()
        copies.append(copy)

    for t in range(tiles):
        stage[t * WPITCH + 3 * MOMENTS : t * WPITCH + WROWS, :] = jnp.zeros((WROWS - 3 * MOMENTS, TILE), jnp.float32)
    rank = lax.rem(lax.broadcasted_iota(jnp.int32, (tiles * FPITCH, TILE), 0), FPITCH)
    row_near[...] = jnp.where((rank > 20) & (rank < 24), 1.0, 0.0)
    col_near[...] = jnp.where((rank > 17) & (rank < 21), 1.0, 0.0)
    col_wide[...] = jnp.where((rank > 23) & (rank < 27), 1.0, 0.0)
    for plane in range(PLANES):
        src_terms[plane * pitch : plane * pitch + tiles, :] = jnp.zeros((tiles, TILE), jnp.float32)
    for k in range(3):
        mean = jnp.sum(row_blk[col, k * tiles : (k + 1) * tiles], keepdims=True) * (1.0 / (tiles * TILE))
        center[k] = jnp.broadcast_to(mean, (tiles, TILE))

    def part(block, at, k):
        return block[at, k * tiles : (k + 1) * tiles]

    def put(out, rows, r, value):
        out[pl.ds(r, tiles, stride=rows), :] = value

    def prepare(block, at, weights, near, wide_near, features, target):
        x = [part(block, at, k) - center[k] for k in range(3)]
        a = [part(block, at, 3 + k) for k in range(3)]
        b = cross(x, a)
        moments = a + b + [p * v for p in x for v in a] + [p * v for p in x for v in b]
        for r, value in enumerate(moments):
            for j, piece in enumerate(thirds(value)):
                put(stage, WPITCH, j * MOMENTS + r, piece)
        sigma = part(block, at, 6)
        half = 0.5 * sigma * sigma
        norm = thirds(dot3(x, x) + half)
        wide = thirds(1.5 * half)
        places = [thirds(value if target else -2.0 * value) for value in x]
        for n, j in enumerate((0, 0, 0, 1, 1, 2) if target else (0, 1, 2, 0, 1, 0)):
            for k in range(3):
                put(near, FPITCH, 3 * n + k, places[k][j])
        for j in range(3):
            put(near, FPITCH, (18 if target else 21) + j, norm[j])
            put(wide_near, FPITCH, (24 if target else 21) + j, wide[j])
        for t in range(tiles):
            weights[at * tiles + t] = stage[t * WPITCH : t * WPITCH + WROWS, :].astype(jnp.bfloat16)
            some = slice(t * FPITCH, t * FPITCH + FROWS)
            features[at * tiles + t, :, 0:TILE] = near[some, :].astype(jnp.bfloat16)
            if not target:
                features[at * tiles + t, :, TILE:] = wide_near[some, :].astype(jnp.bfloat16)

    def prepare_row(k):
        prepare(row_blk, lax.rem(col + ncols - k, ncols), row_w, row_near, row_near, row_f, True)

    def prepare_col(k):
        prepare(col_blk, lax.rem(row + nrows - k, nrows), col_w, col_near, col_wide, col_f, False)

    def keep_terms(terms, s, out):
        for n, (first, at) in enumerate(((0, 0), (0, TILE), (8, TILE), (16, TILE))):
            total = out[first : first + 8, at : at + TILE]
            for j in (1, 2):
                total = total + out[j * MOMENTS + first : j * MOMENTS + first + 8, at : at + TILE]
            terms[pl.ds(n * 8 * pitch + s, 8, stride=pitch), :] = total

    def meet(u, ti, sj):
        near_buf[u] = lax.dot_general(row_f[ti], col_f[sj], (((0,), (0,)), ((), ())), preferred_element_type=jnp.float32)

    def spread(u, react):
        near = near_buf[u]
        for c in range(TILE // CHUNK):
            at = slice(c * CHUNK, (c + 1) * CHUNK)
            at2 = slice(TILE + c * CHUNK, TILE + (c + 1) * CHUNK)
            inv = lax.rsqrt(near[at, 0:TILE])
            inv2 = inv * inv
            ratio = near[at, TILE:] * inv2
            inv3 = inv2 * inv
            q1, q2 = split(inv3 * (ratio + 1.0))
            f1, f2 = split((inv3 * inv2) * (ratio + 0.6))
            tgt_buf[u, at, 0:TILE] = q1
            tgt_buf[u, at, TILE:] = q2
            tgt_buf[u, at2, 0:TILE] = f1
            tgt_buf[u, at2, TILE:] = f2
            if react:
                src_buf[u, at, 0:TILE] = q1
                src_buf[u, at, TILE:] = f1
                src_buf[u, at2, 0:TILE] = q2
                src_buf[u, at2, TILE:] = f2

    def gather(u, s, ti, sj, react):
        some = col_w[sj]
        both = jnp.concatenate([some, some], axis=1)
        out = lax.dot_general(both, tgt_buf[u], (((1,), (1,)), ((), ())), preferred_element_type=jnp.float32)
        keep_terms(tgt_terms, s, out)
        if react:
            some = row_w[ti]
            both = jnp.concatenate([some, some], axis=1)
            out = lax.dot_general(both, src_buf[u], (((1,), (0,)), ((), ())), preferred_element_type=jnp.float32)
            keep_terms(src_terms, s, out)

    def group(places, react):
        for u, (s, ti, sj) in enumerate(places):
            meet(u, ti, sj)
        for u, (s, ti, sj) in enumerate(places):
            spread(u, react)
        for u, (s, ti, sj) in enumerate(places):
            gather(u, s, ti, sj, react)

    prepare_row(0)
    prepare_col(0)

    def diagonal(step, _):
        places = [(step * 4 + u, col * tiles + step * 4 + u, row * tiles + step * 4 + u) for u in range(4)]
        group(places, False)
        return 0

    lax.fori_loop(0, tiles // 4, diagonal, 0)

    def arrived(axis, size, me, block, base, prepare_one):
        def step(k, _):
            other = lax.rem(me + size - k, size)
            place = block.at[other]
            pltpu.make_async_remote_copy(
                src_ref=place,
                dst_ref=place,
                send_sem=send.at[0, base + k - 1],
                recv_sem=recv.at[0, base + k - 1],
                device_id={axis: other},
                device_id_type=MESH,
            ).wait_recv()
            prepare_one(k)
            return 0

        lax.fori_loop(1, size, step, 0)

    arrived("col", ncols, col, row_blk, 0, prepare_row)
    arrived("row", nrows, row, col_blk, ncols - 1, prepare_col)

    def visit(step, _):
        first = tiles + step * UNROLL
        group([(first + u, slots[0, first + u], slots[1, first + u]) for u in range(UNROLL)], True)
        return 0

    lax.fori_loop(0, (num_slots - tiles) // UNROLL, visit, 0)

    first = slot_rows[0:1, :]
    second = slot_rows[1:2, :]
    slot = lax.broadcasted_iota(jnp.int32, (1, num_slots), 1)
    first = jnp.where(slot < tiles, col * tiles + slot, first)
    gi = row * (ncols * tiles) + first
    gj = ((second // tiles) * ncols + col) * tiles + second % tiles
    alive = slot < count[0]
    row_sel = jnp.where(alive, first, -1)
    col_sel = jnp.where(alive & (gi != gj) & (slot >= tiles), second, -1)

    def finish(select, terms, block, out):
        size = block.shape[0] * tiles
        here = lax.broadcasted_iota(jnp.int32, (size, num_slots), 0)
        hot = jnp.where(here == select, 1.0, 0.0)
        hot = jnp.concatenate([hot, hot, hot], axis=1).astype(jnp.bfloat16)
        sums = []
        for n in range(PLANES // 2):
            pieces = [thirds(terms[(2 * n + m) * pitch : (2 * n + m) * pitch + num_slots, :]) for m in range(2)]
            rows = jnp.concatenate([jnp.concatenate([pieces[0][j], pieces[1][j]], axis=1) for j in range(3)], axis=0)
            value = jnp.dot(hot, rows.astype(jnp.bfloat16), preferred_element_type=jnp.float32)
            sums += [value[:, 0:TILE], value[:, TILE:]]
        qa, qb, fa, fb = sums[0:3], sums[3:6], sums[8:11], sums[11:14]
        fxa, fxb = sums[14:23], sums[23:32]
        x = [block[:, k * tiles : (k + 1) * tiles].reshape(size, TILE) - center[k, 0:1] for k in range(3)]
        a = [block[:, (3 + k) * tiles : (4 + k) * tiles].reshape(size, TILE) for k in range(3)]
        velocity = cross(x, qa)
        turn = cross(a, qa)
        along = dot3(a, x)
        spin = cross(x, fa)
        toward = [dot3(a, [fxa[3 * k + m] for k in range(3)]) for m in range(3)]
        swing = cross(x, toward)
        for k in range(3):
            steep = along * (spin[k] - fb[k]) - swing[k] + dot3(a, [fxb[3 * m + k] for m in range(3)])
            v = biot_factor * (velocity[k] - qb[k])
            w = biot_factor * (turn[k] - 5.0 * steep)
            out[:, k] = v.reshape(size // tiles, tiles, TILE)
            out[:, 3 + k] = w.reshape(size // tiles, tiles, TILE)

    for copy in copies:
        copy.wait_send()

    def send_all(axis, first_sem, size, me, sums, held):
        started = []
        for k in range(1, size):
            other = lax.rem(me + k, size)
            copy = pltpu.make_async_remote_copy(
                src_ref=sums.at[other],
                dst_ref=held.at[k - 1],
                send_sem=send.at[1, first_sem + k - 1],
                recv_sem=recv.at[1, first_sem + k - 1],
                device_id={axis: other},
                device_id_type=MESH,
            )
            copy.start()
            started.append((copy, held.at[k - 1]))
        return started

    finish(row_sel, tgt_terms, row_blk, row_sum)
    started = send_all("col", 0, ncols, col, row_sum, row_held)
    finish(col_sel, src_terms, col_blk, col_sum)
    started += send_all("row", ncols - 1, nrows, row, col_sum, col_held)
    total = row_sum[col] + col_sum[row]
    for copy, held in started:
        copy.wait_recv()
        total = total + held[...]
    for t in range(tiles):
        part = slice(t * TILE, (t + 1) * TILE)
        live = lane[0:1, :] < counts[t]
        for k in range(3):
            sums_out[k : k + 1, part] = jnp.where(live, total[k, t : t + 1, :], 0.0)
            sums_out[3 + k : 4 + k, part] = jnp.where(live, total[3 + k, t : t + 1, :], 0.0)
    for copy, _ in started:
        copy.wait_send()


def shards(nrows, ncols, positions, strengths, cores, order, tile_counts, pair_slots, pair_count):
    tiles = tile_counts.shape[0]
    num_slots = pair_slots.shape[1]
    others = nrows + ncols - 2
    nt, ns = ncols * tiles, nrows * tiles
    f32, bf16 = jnp.float32, jnp.bfloat16
    sums = pl.pallas_call(
        functools.partial(wake_kernel, nrows, ncols, tiles),
        out_shape=pltpu.VMEM((6, tiles * TILE), f32),
        in_specs=[HBM] * 7,
        out_specs=VMEM,
        scratch_shapes=[
            pltpu.SMEM((2, num_slots), jnp.int32),
            pltpu.SMEM((1,), jnp.int32),
            pltpu.SMEM((tiles,), jnp.int32),
            pltpu.VMEM((2, num_slots), jnp.int32),
            pltpu.VMEM((3, tiles * TILE), f32),
            pltpu.VMEM((3, tiles * TILE), f32),
            pltpu.VMEM((tiles, TILE), f32),
            pltpu.VMEM((tiles, TILE), jnp.int32),
            pltpu.VMEM((tiles, 8, TILE), f32),
            pltpu.VMEM((ncols, 7 * tiles, TILE), f32),
            pltpu.VMEM((nrows, 7 * tiles, TILE), f32),
            pltpu.VMEM((3, tiles, TILE), f32),
            pltpu.VMEM((tiles * WPITCH, TILE), f32),
            pltpu.VMEM((tiles * FPITCH, TILE), f32),
            pltpu.VMEM((tiles * FPITCH, TILE), f32),
            pltpu.VMEM((tiles * FPITCH, TILE), f32),
            pltpu.VMEM((nt, WROWS, TILE), bf16),
            pltpu.VMEM((ns, WROWS, TILE), bf16),
            pltpu.VMEM((nt, FROWS, TILE), bf16),
            pltpu.VMEM((ns, FROWS, 2 * TILE), bf16),
            pltpu.VMEM((UNROLL, TILE, 2 * TILE), f32),
            pltpu.VMEM((UNROLL, 2 * TILE, 2 * TILE), bf16),
            pltpu.VMEM((UNROLL, 2 * TILE, 2 * TILE), bf16),
            pltpu.VMEM((PLANES * (num_slots + 4), TILE), f32),
            pltpu.VMEM((PLANES * (num_slots + 4), TILE), f32),
            pltpu.VMEM((ncols, 6, tiles, TILE), f32),
            pltpu.VMEM((nrows, 6, tiles, TILE), f32),
            pltpu.VMEM((ncols - 1, 6, tiles, TILE), f32),
            pltpu.VMEM((nrows - 1, 6, tiles, TILE), f32),
            pltpu.SemaphoreType.DMA((8,)),
            pltpu.SemaphoreType.DMA((2, others)),
            pltpu.SemaphoreType.DMA((2, others)),
        ],
        compiler_params=pltpu.CompilerParams(
            collective_id=0, has_side_effects=True, vmem_limit_bytes=56 * 1024 * 1024
        ),
        name="wake",
    )(pair_count, tile_counts, pair_slots, positions, strengths,
      cores.reshape(tiles, TILE), order.reshape(tiles, TILE))
    return sums[0:3], sums[3:6]


def solution(mesh):
    whole = ("groups", "row", "col")
    in_specs = (P(None, whole), P(None, whole), P(whole), P(whole), P(whole), P(None, whole), P(whole))
    out_specs = (P(None, whole), P(None, whole))
    body = functools.partial(shards, mesh.shape["row"], mesh.shape["col"])
    return jax.shard_map(body, mesh=mesh, in_specs=in_specs, out_specs=out_specs, check_vma=False)
```
